32 devices in a mesh: pos: 8 (over z, x), exp: 4 (over y, core).
Axes of the slice: x: 2, y: 2, z: 4, core: 2. Of those that a mesh axis runs over, the one named last changes fastest.
Arguments:
- patches: bfloat16 [8192, 4, 256], P(('pos', 'exp')), may hold values from -6 to 6
- conv_weight: bfloat16 [3, 256, 2048], replicated, may hold values from -0.21875 to 0.21875
- phi: bfloat16 [2048, 32], replicated, may hold values from -40 to 40, as said below
- w_in: bfloat16 [4, 2048, 8192], P('exp', None, 'pos'), may hold values from -0.125 to 0.125
- w_out: bfloat16 [4, 8192, 2048], P('exp', 'pos'), may hold values from -0.0625 to 0.0625
Outputs:
- mixed: bfloat16 [8192, 4, 2048], P(('pos', 'exp'))
The draws below stay inside these ranges and needn't reach their ends.
Inputs may be any that keep to these rules, and one draw needn't show every extreme that they name: phi is real-valued.
All inputs are finite; a program needn't handle non-finite values.
Results may differ from the reference program's by a relative error of at most 0.019.
The reference program's roundings to bfloat16 on the way (of `tokens`, `dispatch`, `slot_in`, `hidden`, `slot_out` and `combine`) count: a program that leaves them out, or rounds other values in their place, can miss the bound.
Values may be sent and summed in bfloat16 or wider, within the bound.
A program may use at most 128 MiB of HBM per device.

```python
import math
import jax
import jax.numpy as jnp
from jax import lax

D = 2048
FF = 8192
PATCH = 256
SLOTS_PER = 8
TP = 4
CH = 8192
EXPERTS = 4
SLOTS = 32


def draw_phi(key, part):
    first_key, second_key = jax.random.split(key, 2)
    base = jnp.clip(jax.random.normal(first_key, (D, SLOTS), jnp.float32), -5.0, 5.0)
    scale = jnp.exp(jax.random.uniform(second_key, (1, SLOTS), jnp.float32, math.log(3.0), math.log(4.5)))
    return jnp.clip(base * scale * (2.0 / math.sqrt(D)), -40.0, 40.0).astype(jnp.bfloat16)


def level_of(own_key, extent, cuts, least, largest):
    loudness = 1.0
    for dim, parts in cuts:
        draws = jax.random.uniform(jax.random.fold_in(jax.random.fold_in(own_key, 6), dim), (parts,), jnp.float32, least / len(cuts), largest / len(cuts))
        loudness = loudness * jnp.repeat(jnp.exp(draws), extent[dim] // parts).reshape((-1,) + (1,) * (len(extent) - 1 - dim))
    return loudness


def normal_values(own_key, dims, scale, limit, shards=(), kind=jnp.bfloat16):
    drawn = jax.random.normal(own_key, dims, jnp.float32) * scale
    if len(shards) > 0:
        drawn = level_of(own_key, dims, shards, -0.22, 0.18) * drawn
    return jnp.clip(drawn, min=-limit, max=limit).astype(kind)


def setup_inputs(seed: int = 0) -> dict:
    key_of = jax.random.split(jax.random.key(seed), 6)
    patches = normal_values(key_of[0], (CH, TP, PATCH), 1.0, 6.0, ((0, 32),))
    conv_weight = normal_values(key_of[1], (3, PATCH, D), (3 * PATCH) ** -0.5, 0.21875)
    phi = draw_phi(jax.random.fold_in(key_of[5], 71), 0)
    w_in = normal_values(key_of[3], (EXPERTS, D, FF), D ** -0.5, 0.125, ((0, 4), (2, 8)))
    w_out = normal_values(key_of[4], (EXPERTS, FF, D), FF ** -0.5, 0.0625, ((0, 4), (1, 8)))
    return dict(patches=patches, conv_weight=conv_weight, phi=phi, w_in=w_in, w_out=w_out)


def reference(patches, conv_weight, phi, w_in, w_out):
    padded = jnp.pad(patches, ((1, 1), (0, 0), (0, 0)))

    def encode(channel):
        rows = lax.dynamic_slice_in_dim(padded, channel, 3, 0)
        running = jnp.zeros((TP, D), jnp.float32)
        for offset in range(3):
            running = running + jnp.dot(rows[offset], conv_weight[offset], preferred_element_type=jnp.float32)
        return running.astype(jnp.bfloat16)

    tokens = lax.map(encode, jnp.arange(CH, dtype=jnp.int32))
    flat = tokens.reshape(CH * TP, D)
    logits = jnp.dot(flat, phi, preferred_element_type=jnp.float32)
    column_peak = jnp.max(logits, axis=0)
    raw_weights = jnp.exp(logits - column_peak)
    column_total = jnp.sum(raw_weights, axis=0)
    dispatch = (raw_weights / column_total).astype(jnp.bfloat16)
    slot_in = lax.dot_general(dispatch, flat, (((0,), (0,)), ((), ())), preferred_element_type=jnp.float32).astype(jnp.bfloat16)

    def expert(inputs):
        rows, first, second = inputs
        hidden = jax.nn.gelu(jnp.dot(rows, first, preferred_element_type=jnp.float32), approximate=True).astype(jnp.bfloat16)
        return jnp.dot(hidden, second, preferred_element_type=jnp.float32).astype(jnp.bfloat16)

    slot_out = lax.map(expert, (slot_in.reshape(EXPERTS, SLOTS_PER, D), w_in, w_out)).reshape(SLOTS, D)
    row_peak = jnp.max(logits, axis=1, keepdims=True)
    row_weights = jnp.exp(logits - row_peak)
    combine = (row_weights / jnp.sum(row_weights, axis=1, keepdims=True)).astype(jnp.bfloat16)
    mixed = jnp.dot(combine, slot_out, preferred_element_type=jnp.float32).astype(jnp.bfloat16)
    return mixed.reshape(CH, TP, D)
```

```python
import functools

import jax
import jax.numpy as jnp
from jax import lax
from jax.experimental import pallas as pl
from jax.experimental.pallas import tpu as pltpu
from jax.sharding import PartitionSpec as P

MESH = pl.DeviceIdType.MESH
F32 = jnp.float32
BF16 = jnp.bfloat16


def pack(block):
    rows, width = block.shape
    if width % 256 == 0:
        half = width // 2
        return jnp.concatenate([block[:, :half], block[:, half:]], axis=0).astype(BF16)
    return jnp.concatenate([block, jnp.zeros_like(block)], axis=0).astype(BF16)


def packed_shape(rows, width):
    return (2 * rows, width // 2 if width % 256 == 0 else width)


def unpack(block, width):
    wide = block.astype(F32)
    rows = wide.shape[0] // 2
    if width % 256 == 0:
        return jnp.concatenate([wide[:rows], wide[rows:]], axis=1)
    return wide[:rows]


def layer_kernel(
    n_pos, n_exp, chunk,
    patches, taps, phi_t, w_in, w_out,
    combine_ref, slots_ref,
    x_raw, xs, taps_v, phi_v, win_v, wout_v, tokens, logits,
    halo_out, halo_in,
    stat_own, stat_exp, stat_mid, stat_pos,
    sum_own, sum_out, sum_exp,
    part_own, part_out, part_pos,
    in_own, in_all,
    term_own, term_out, term_pos,
    out_all,
    local_sem, chunk_sem,
    halo_s, halo_r, stat_es, stat_er, stat_ps, stat_pr,
    sum_s, sum_r, part_s, part_r, in_s, in_r, term_s, term_r,
    slot_s, slot_r, far_s, far_r,
):
    p, e = lax.axis_index("pos"), lax.axis_index("exp")
    count = n_pos * n_exp
    g = p * n_exp + e
    channels, periods, samples = x_raw.shape
    rows = channels * periods
    d = tokens.shape[1]
    n_slots = phi_v.shape[0]
    per = n_slots // n_exp
    blk = d // n_pos
    n_chunks = d // chunk
    edge = rows // 4

    right, left = lax.rem(g + 1, count), lax.rem(g + count - 1, count)
    right_id = (right // n_exp, lax.rem(right, n_exp))
    left_id = (left // n_exp, lax.rem(left, n_exp))
    exp_ids = [(p, lax.rem(e + k, n_exp)) for k in range(1, n_exp)]
    pos_ids = [(lax.rem(p + k, n_pos), e) for k in range(1, n_pos)]

    barrier = pltpu.get_barrier_semaphore()
    for device in [right_id, left_id] + exp_ids + pos_ids:
        pl.semaphore_signal(barrier, inc=1, device_id=device, device_id_type=MESH)

    def send(src, dst, s, r, device):
        copy = pltpu.make_async_remote_copy(
            src_ref=src, dst_ref=dst, send_sem=s, recv_sem=r,
            device_id=device, device_id_type=MESH,
        )
        copy.start()
        return copy

    x_copy = pltpu.make_async_copy(patches, x_raw, local_sem.at[0])
    x_copy.start()

    def tap_copy(n):
        cols = pl.ds(pl.multiple_of(n * chunk, chunk), chunk)
        return pltpu.make_async_copy(taps.at[:, cols], taps_v.at[:, cols], chunk_sem.at[n])

    for n in range(n_chunks):
        tap_copy(n).start()
    phi_copy = pltpu.make_async_copy(phi_t, phi_v, local_sem.at[1])
    phi_copy.start()

    x_copy.wait()
    x = x_raw[...].astype(F32).reshape(rows, samples)
    halo_out[0] = x[rows - 8 :]
    halo_out[1] = x[:8]
    xs[:, samples : 2 * samples] = x.astype(BF16)
    up = pltpu.roll(x, periods, 0)
    down = pltpu.roll(x, rows - periods, 0)
    xs[:, :samples] = up.astype(BF16)
    xs[:, 2 * samples :] = down.astype(BF16)

    pl.semaphore_wait(barrier, 2 + (n_exp - 1) + (n_pos - 1))
    halo = [
        send(halo_out.at[0], halo_in.at[0], halo_s.at[0], halo_r.at[0], right_id),
        send(halo_out.at[1], halo_in.at[1], halo_s.at[1], halo_r.at[1], left_id),
    ]

    def encode(n, begin, length):
        cols = pl.ds(pl.multiple_of(n * chunk, chunk), chunk)
        tokens[pl.ds(begin, length), cols] = jnp.dot(
            xs[pl.ds(begin, length), :], taps_v[:, cols], preferred_element_type=F32
        ).astype(BF16)

    @pl.loop(0, n_chunks)
    def _(n):
        tap_copy(n).wait()
        encode(n, edge, rows - 2 * edge)

    win_copy = pltpu.make_async_copy(w_in.at[0], win_v, local_sem.at[2])
    win_copy.start()
    wout_copy = pltpu.make_async_copy(w_out.at[0], wout_v, local_sem.at[3])
    wout_copy.start()

    for copy in halo:
        copy.wait()
    row16 = lax.broadcasted_iota(jnp.int32, (16, samples), 0)
    zero8 = jnp.zeros((8, samples), F32)
    before = jnp.concatenate([pltpu.roll(halo_in[0], 4, 0), zero8], axis=0)
    before = jnp.where(g == 0, 0.0, before)
    xs[0:16, :samples] = jnp.where(
        row16 < periods, before, xs[0:16, :samples].astype(F32)
    ).astype(BF16)
    after = jnp.concatenate([zero8, pltpu.roll(halo_in[1], 4, 0)], axis=0)
    after = jnp.where(g == count - 1, 0.0, after)
    xs[rows - 16 :, 2 * samples :] = jnp.where(
        row16 >= 16 - periods, after, xs[rows - 16 :, 2 * samples :].astype(F32)
    ).astype(BF16)

    @pl.loop(0, n_chunks)
    def _(n):
        encode(n, 0, edge)
        encode(n, rows - edge, edge)

    phi_copy.wait()
    contract_last = (((1,), (1,)), ((), ()))
    lg = lax.dot_general(tokens[...], phi_v[...], contract_last, preferred_element_type=F32)
    logits[...] = lg
    lt = lg.T
    peak = jnp.max(lt, axis=1, keepdims=True)
    weights = jnp.exp(lt - peak)
    total = jnp.sum(weights, axis=1, keepdims=True)
    lane = lax.broadcasted_iota(jnp.int32, (n_slots, 128), 1)
    stats = jnp.where(lane < 64, peak, total)
    for q in range(n_exp):
        stat_own[q] = stats[q * per : (q + 1) * per]
    stat_copies = [
        send(stat_own.at[ids[1]], stat_exp.at[k], stat_es.at[k], stat_er.at[k], ids)
        for k, ids in enumerate(exp_ids)
    ]
    sums = jnp.dot(weights.astype(BF16), tokens[...], preferred_element_type=F32)
    for q in range(n_exp):
        own = sums[q * per : (q + 1) * per]
        sum_own[q] = own
        sum_out[q] = pack(own)
    sum_copies = [
        send(sum_out.at[ids[1]], sum_exp.at[k], sum_s.at[k], sum_r.at[k], ids)
        for k, ids in enumerate(exp_ids)
    ]

    def merge(blocks):
        peaks = [b[:, 0:1] for b in blocks]
        totals = [b[:, 64:65] for b in blocks]
        top = functools.reduce(jnp.maximum, peaks)
        scales = [jnp.exp(v - top) for v in peaks]
        whole = functools.reduce(jnp.add, [s * t for s, t in zip(scales, totals)])
        return top, scales, whole

    for copy in stat_copies:
        copy.wait()
    top_e, scales_e, total_e = merge([stat_own[e]] + [stat_exp[k] for k in range(n_exp - 1)])
    lane8 = lax.broadcasted_iota(jnp.int32, (per, 128), 1)
    stat_mid[...] = jnp.where(lane8 < 64, top_e, total_e)
    stat_copies = [
        send(stat_mid, stat_pos.at[k], stat_ps.at[k], stat_pr.at[k], ids)
        for k, ids in enumerate(pos_ids)
    ]

    lg = logits[...]
    row_weights = jnp.exp(lg - jnp.max(lg, axis=1, keepdims=True))
    combine_ref[...] = (
        row_weights / jnp.sum(row_weights, axis=1, keepdims=True)
    ).astype(BF16)

    for copy in stat_copies:
        copy.wait()
    top, scales_p, total_all = merge([stat_mid[...]] + [stat_pos[k] for k in range(n_pos - 1)])
    factor = scales_p[0] / total_all

    for copy in sum_copies:
        copy.wait()
    part = scales_e[0] * sum_own[e]
    for k in range(n_exp - 1):
        part = part + scales_e[k + 1] * unpack(sum_exp[k], d)
    part = factor * part
    for q in range(n_pos):
        block = part[:, q * blk : (q + 1) * blk]
        part_own[q] = block
        part_out[q] = pack(block)
    part_copies = [
        send(part_out.at[ids[0]], part_pos.at[k], part_s.at[k], part_r.at[k], ids)
        for k, ids in enumerate(pos_ids)
    ]
    for copy in part_copies:
        copy.wait()
    mine = part_own[p]
    for k in range(n_pos - 1):
        mine = mine + unpack(part_pos[k], blk)
    in_own[...] = pack(mine)
    in_copies = [
        send(in_own, in_all.at[p], in_s.at[k], in_r.at[k], ids)
        for k, ids in enumerate(pos_ids)
    ]
    in_all[p] = in_own[...]
    win_copy.wait()
    for copy in in_copies:
        copy.wait()
    slot_in = jnp.concatenate(
        [unpack(in_all[q], blk) for q in range(n_pos)], axis=1
    ).astype(BF16)
    hidden = jax.nn.gelu(
        jnp.dot(slot_in, win_v[...], preferred_element_type=F32), approximate=True
    ).astype(BF16)
    wout_copy.wait()
    term = jnp.dot(hidden, wout_v[...], preferred_element_type=F32)
    for q in range(n_pos):
        block = term[:, q * blk : (q + 1) * blk]
        term_own[q] = block
        term_out[q] = pack(block)
    term_copies = [
        send(term_out.at[ids[0]], term_pos.at[k], term_s.at[k], term_r.at[k], ids)
        for k, ids in enumerate(pos_ids)
    ]
    for copy in term_copies:
        copy.wait()
    mine = term_own[p]
    for k in range(n_pos - 1):
        mine = mine + unpack(term_pos[k], blk)
    out_all[e, p] = pack(mine)
    slot_copies = [
        send(out_all.at[e, p], out_all.at[e, p], slot_s.at[k], slot_r.at[k], ids)
        for k, ids in enumerate(pos_ids)
    ]
    for copy in slot_copies:
        copy.wait()
    far_copies = [
        send(out_all.at[e], out_all.at[e], far_s.at[k], far_r.at[k], ids)
        for k, ids in enumerate(exp_ids)
    ]
    for copy in far_copies:
        copy.wait()
    slots_ref[...] = jnp.concatenate(
        [
            jnp.concatenate([unpack(out_all[i, q], blk) for q in range(n_pos)], axis=1)
            for i in range(n_exp)
        ],
        axis=0,
    ).astype(BF16)


def mix_kernel(combine_ref, slots_ref, out_ref):
    mixed = jnp.dot(combine_ref[...], slots_ref[...], preferred_element_type=F32)
    out_ref[...] = mixed.astype(BF16).reshape(out_ref.shape)


def per_device(n_pos, n_exp, patches, conv_weight, phi, w_in, w_out):
    channels, periods, samples = patches.shape
    rows = channels * periods
    d, n_slots = phi.shape
    ff = w_in.shape[2]
    per = n_slots // n_exp
    blk = d // n_pos
    chunk = 512
    wide, narrow = packed_shape(per, d), packed_shape(per, blk)
    dma = lambda *shape: pltpu.SemaphoreType.DMA(shape)
    any_spec = pl.BlockSpec(memory_space=pl.ANY)
    vmem_spec = pl.BlockSpec(memory_space=pltpu.VMEM)
    pairs = [2, 2, n_exp - 1, n_exp - 1, n_pos - 1, n_pos - 1, n_exp - 1, n_exp - 1]
    pairs += [n_pos - 1] * 8 + [n_exp - 1] * 2
    combine, slots = pl.pallas_call(
        functools.partial(layer_kernel, n_pos, n_exp, chunk),
        out_shape=(
            jax.ShapeDtypeStruct((rows, n_slots), BF16),
            jax.ShapeDtypeStruct((n_slots, d), BF16),
        ),
        in_specs=[any_spec] * 5,
        out_specs=(vmem_spec, vmem_spec),
        scratch_shapes=[
            pltpu.VMEM((channels, periods, samples), BF16),
            pltpu.VMEM((rows, 3 * samples), BF16),
            pltpu.VMEM((3 * samples, d), BF16),
            pltpu.VMEM((n_slots, d), BF16),
            pltpu.VMEM((d, ff), BF16),
            pltpu.VMEM((ff, d), BF16),
            pltpu.VMEM((rows, d), BF16),
            pltpu.VMEM((rows, n_slots), F32),
            pltpu.VMEM((2, 8, samples), F32),
            pltpu.VMEM((2, 8, samples), F32),
            pltpu.VMEM((n_exp, per, 128), F32),
            pltpu.VMEM((n_exp - 1, per, 128), F32),
            pltpu.VMEM((per, 128), F32),
            pltpu.VMEM((n_pos - 1, per, 128), F32),
            pltpu.VMEM((n_exp, per, d), F32),
            pltpu.VMEM((n_exp,) + wide, BF16),
            pltpu.VMEM((n_exp - 1,) + wide, BF16),
            pltpu.VMEM((n_pos, per, blk), F32),
            pltpu.VMEM((n_pos,) + narrow, BF16),
            pltpu.VMEM((n_pos - 1,) + narrow, BF16),
            pltpu.VMEM(narrow, BF16),
            pltpu.VMEM((n_pos,) + narrow, BF16),
            pltpu.VMEM((n_pos, per, blk), F32),
            pltpu.VMEM((n_pos,) + narrow, BF16),
            pltpu.VMEM((n_pos - 1,) + narrow, BF16),
            pltpu.VMEM((n_exp, n_pos) + narrow, BF16),
            dma(4),
            dma(d // chunk),
        ]
        + [dma(c) for c in pairs],
        compiler_params=pltpu.CompilerParams(
            collective_id=0, has_side_effects=True, vmem_limit_bytes=48 * 2**20
        ),
        name="moe_layer",
    )(patches, conv_weight.reshape(3 * samples, d), phi.T, w_in, w_out)
    step = 32
    return pl.pallas_call(
        mix_kernel,
        grid=(channels // step,),
        out_shape=jax.ShapeDtypeStruct((channels, periods, d), BF16),
        in_specs=[
            pl.BlockSpec((step * periods, n_slots), lambda i: (i, 0)),
            pl.BlockSpec((n_slots, d), lambda i: (0, 0)),
        ],
        out_specs=pl.BlockSpec((step, periods, d), lambda i: (i, 0, 0)),
        compiler_params=pltpu.CompilerParams(vmem_limit_bytes=32 * 2**20),
        name="mix_slots",
    )(combine, slots)


def solution(mesh):
    in_specs = (
        P(("pos", "exp"), None, None),
        P(),
        P(),
        P("exp", None, "pos"),
        P("exp", "pos", None),
    )
    out_specs = P(("pos", "exp"), None, None)
    body = functools.partial(per_device, mesh.shape["pos"], mesh.shape["exp"])
    return jax.shard_map(
        body, mesh=mesh, in_specs=in_specs, out_specs=out_specs, check_vma=False
    )
```

```python
import functools

import jax
import jax.numpy as jnp
from jax import lax
from jax.experimental import pallas as pl
from jax.experimental.pallas import tpu as pltpu
from jax.sharding import PartitionSpec as P

MESH = pl.DeviceIdType.MESH
F32 = jnp.float32
BF16 = jnp.bfloat16
FOLD = 2


def pack(block):
    rows, width = block.shape
    if width % 256 == 0:
        half = width // 2
        return jnp.concatenate([block[:, :half], block[:, half:]], axis=0).astype(BF16)
    return jnp.concatenate([block, jnp.zeros_like(block)], axis=0).astype(BF16)


def packed_shape(rows, width):
    return (2 * rows, width // 2 if width % 256 == 0 else width)


def unpack(block, width):
    wide = block.astype(F32)
    rows = wide.shape[0] // 2
    if width % 256 == 0:
        return jnp.concatenate([wide[:rows], wide[rows:]], axis=1)
    return wide[:rows]


def layer_kernel(
    n_pos, n_exp, chunk,
    patches, taps, phi_t, w_in, w_out,
    combine_ref, slots_ref,
    x_raw, xs, taps_v, phi_v, win_v, wout_v, tokens,
    halo_out, halo_in,
    stat_own, stat_plane, stat_z,
    sum_own, sum_out, sum_plane,
    in_all,
    term_out, term_pos,
    out_all, slots_v,
    local_sem, chunk_sem,
    halo_s, halo_r, stat_es, stat_er, stat_ps, stat_pr,
    sum_s, sum_r, in_s, in_r, term_s, term_r,
    slot_s, slot_r,
):
    p, e = lax.axis_index("pos"), lax.axis_index("exp")
    count = n_pos * n_exp
    g = p * n_exp + e
    channels, periods, samples = x_raw.shape
    rows = channels * periods
    d = tokens.shape[1]
    n_slots = phi_v.shape[0]
    per = n_slots // n_exp
    half = d // FOLD
    n_chunks = d // chunk
    edge = rows // 4

    right, left = lax.rem(g + 1, count), lax.rem(g + count - 1, count)
    right_id = (right // n_exp, lax.rem(right, n_exp))
    left_id = (left // n_exp, lax.rem(left, n_exp))
    z, x = p // FOLD, lax.rem(p, FOLD)
    n_z = n_pos // FOLD
    plane = [(a, b) for a in range(FOLD) for b in range(n_exp) if (a, b) != (0, 0)]
    plane_xe = [(lax.rem(x + a, FOLD), lax.rem(e + b, n_exp)) for a, b in plane]
    plane_ids = [(z * FOLD + a, b) for a, b in plane_xe]
    pos_p = [lax.rem(p + k, n_pos) for k in range(1, n_pos)]
    pos_ids = [(q, e) for q in pos_p]
    z_ids = [(lax.rem(z + k, n_z) * FOLD + x, e) for k in range(1, n_z)]

    barrier = pltpu.get_barrier_semaphore()
    for device in [right_id, left_id] + plane_ids + pos_ids:
        pl.semaphore_signal(barrier, inc=1, device_id=device, device_id_type=MESH)

    def send(src, dst, s, r, device):
        copy = pltpu.make_async_remote_copy(
            src_ref=src, dst_ref=dst, send_sem=s, recv_sem=r,
            device_id=device, device_id_type=MESH,
        )
        copy.start()
        return copy

    x_copy = pltpu.make_async_copy(patches, x_raw, local_sem.at[0])
    x_copy.start()

    def tap_copy(n):
        cols = pl.ds(pl.multiple_of(n * chunk, chunk), chunk)
        return pltpu.make_async_copy(taps.at[:, cols], taps_v.at[:, cols], chunk_sem.at[n])

    for n in range(n_chunks):
        tap_copy(n).start()
    phi_copy = pltpu.make_async_copy(phi_t, phi_v, local_sem.at[1])
    phi_copy.start()

    x_copy.wait()
    raw = x_raw[...].astype(F32).reshape(rows, samples)
    halo_out[0] = raw[rows - 8 :]
    halo_out[1] = raw[:8]
    xs[:, samples : 2 * samples] = raw.astype(BF16)
    up = pltpu.roll(raw, periods, 0)
    down = pltpu.roll(raw, rows - periods, 0)
    xs[:, :samples] = up.astype(BF16)
    xs[:, 2 * samples :] = down.astype(BF16)

    pl.semaphore_wait(barrier, 2 + len(plane_ids) + len(pos_ids))
    halo = [
        send(halo_out.at[0], halo_in.at[0], halo_s.at[0], halo_r.at[0], right_id),
        send(halo_out.at[1], halo_in.at[1], halo_s.at[1], halo_r.at[1], left_id),
    ]

    def encode(n, begin, length):
        cols = pl.ds(pl.multiple_of(n * chunk, chunk), chunk)
        tokens[pl.ds(begin, length), cols] = jnp.dot(
            xs[pl.ds(begin, length), :], taps_v[:, cols], preferred_element_type=F32
        ).astype(BF16)

    @pl.loop(0, n_chunks)
    def _(n):
        tap_copy(n).wait()
        encode(n, edge, rows - 2 * edge)

    win_copy = pltpu.make_async_copy(w_in.at[0], win_v, local_sem.at[2])
    win_copy.start()
    wout_copy = pltpu.make_async_copy(w_out.at[0], wout_v, local_sem.at[3])
    wout_copy.start()

    for copy in halo:
        copy.wait()
    row16 = lax.broadcasted_iota(jnp.int32, (16, samples), 0)
    zero8 = jnp.zeros((8, samples), F32)
    before = jnp.concatenate([pltpu.roll(halo_in[0], 4, 0), zero8], axis=0)
    before = jnp.where(g == 0, 0.0, before)
    xs[0:16, :samples] = jnp.where(
        row16 < periods, before, xs[0:16, :samples].astype(F32)
    ).astype(BF16)
    after = jnp.concatenate([zero8, pltpu.roll(halo_in[1], 4, 0)], axis=0)
    after = jnp.where(g == count - 1, 0.0, after)
    xs[rows - 16 :, 2 * samples :] = jnp.where(
        row16 >= 16 - periods, after, xs[rows - 16 :, 2 * samples :].astype(F32)
    ).astype(BF16)

    @pl.loop(0, n_chunks)
    def _(n):
        encode(n, 0, edge)
        encode(n, rows - edge, edge)

    phi_copy.wait()
    contract_last = (((1,), (1,)), ((), ()))
    lt = lax.dot_general(phi_v[...], tokens[...], contract_last, preferred_element_type=F32)
    peak = jnp.max(lt, axis=1, keepdims=True)
    weights = jnp.exp(lt - peak)
    total = jnp.sum(weights, axis=1, keepdims=True)
    lane = lax.broadcasted_iota(jnp.int32, (n_slots, 128), 1)
    stats = jnp.where(lane < 64, peak, total)
    for q in range(n_exp):
        stat_own[q] = stats[q * per : (q + 1) * per]
    stat_copies = [
        send(stat_own.at[to[1]], stat_plane.at[k], stat_es.at[k], stat_er.at[k], to)
        for k, to in enumerate(plane_ids)
    ]
    sums = jnp.dot(weights.astype(BF16), tokens[...], preferred_element_type=F32)
    for q in range(n_exp):
        for f in range(FOLD):
            own = sums[q * per : (q + 1) * per, f * half : (f + 1) * half]
            sum_own[f, q] = own
            sum_out[f, q] = pack(own)
    sum_copies = [
        send(sum_out.at[a, b], sum_plane.at[k], sum_s.at[k], sum_r.at[k], to)
        for k, ((a, b), to) in enumerate(zip(plane_xe, plane_ids))
    ]

    def merge(blocks):
        peaks = [b[:, 0:1] for b in blocks]
        totals = [b[:, 64:65] for b in blocks]
        top = functools.reduce(jnp.maximum, peaks)
        scales = [jnp.exp(v - top) for v in peaks]
        whole = functools.reduce(jnp.add, [s * t for s, t in zip(scales, totals)])
        return top, scales, whole

    for copy in stat_copies:
        copy.wait()
    top_p, scales_p, total_p = merge(
        [stat_own[e]] + [stat_plane[k] for k in range(len(plane_ids))]
    )
    lane8 = lax.broadcasted_iota(jnp.int32, (per, 128), 1)
    stat_z[z] = jnp.where(lane8 < 64, top_p, total_p)
    z_copies = [
        send(stat_z.at[z], stat_z.at[z], stat_ps.at[k], stat_pr.at[k], to)
        for k, to in enumerate(z_ids)
    ]

    row_weights = jnp.exp(lt - jnp.max(lt, axis=0, keepdims=True))
    combine = row_weights / jnp.sum(row_weights, axis=0, keepdims=True)
    combine_ref[...] = combine.T.astype(BF16)

    for copy in sum_copies:
        copy.wait()
    part = scales_p[0] * sum_own[x, e]
    for k in range(len(plane_ids)):
        part = part + scales_p[k + 1] * unpack(sum_plane[k], half)
    in_all[p] = pack(part)
    in_copies = [
        send(in_all.at[p], in_all.at[p], in_s.at[k], in_r.at[k], to)
        for k, to in enumerate(pos_ids)
    ]
    for copy in z_copies:
        copy.wait()
    top, scales_z, total_all = merge([stat_z[q] for q in range(n_z)])
    factors = [s / total_all for s in scales_z]
    win_copy.wait()
    for copy in in_copies:
        copy.wait()

    def gathered(f):
        terms = [factors[q] * unpack(in_all[q * FOLD + f], half) for q in range(n_z)]
        return functools.reduce(jnp.add, terms)

    slot_in = jnp.concatenate([gathered(f) for f in range(FOLD)], axis=1).astype(BF16)
    hidden = jax.nn.gelu(
        jnp.dot(slot_in, win_v[...], preferred_element_type=F32), approximate=True
    ).astype(BF16)
    wout_copy.wait()
    term = jnp.dot(hidden, wout_v[...], preferred_element_type=F32)
    for f in range(FOLD):
        term_out[f] = pack(term[:, f * half : (f + 1) * half])
    term_copies = [
        send(term_out.at[lax.rem(q, FOLD)], term_pos.at[p], term_s.at[k], term_r.at[k], to)
        for k, (q, to) in enumerate(zip(pos_p, pos_ids))
    ]
    term_pos[p] = term_out[x]
    for copy in term_copies:
        copy.wait()
    mine = functools.reduce(jnp.add, [unpack(term_pos[q], half) for q in range(n_pos)])
    out_all[e, x] = pack(mine)
    slot_copies = [
        send(out_all.at[e, x], out_all.at[e, x], slot_s.at[k], slot_r.at[k], to)
        for k, to in enumerate(plane_ids)
    ]
    for copy in slot_copies:
        copy.wait()
    for i in range(n_exp):
        for f in range(FOLD):
            slots_v[i * per : (i + 1) * per, f * half : (f + 1) * half] = unpack(
                out_all[i, f], half
            )
    slots_ref[...] = slots_v[...].astype(BF16)


def mix_kernel(combine_ref, slots_ref, out_ref):
    mixed = jnp.dot(combine_ref[...], slots_ref[...], preferred_element_type=F32)
    out_ref[...] = mixed.astype(BF16).reshape(out_ref.shape)


def per_device(n_pos, n_exp, patches, conv_weight, phi, w_in, w_out):
    channels, periods, samples = patches.shape
    rows = channels * periods
    d, n_slots = phi.shape
    ff = w_in.shape[2]
    per = n_slots // n_exp
    half = d // FOLD
    chunk = 512
    packed = packed_shape(per, half)
    n_plane = n_exp * FOLD - 1
    dma = lambda *shape: pltpu.SemaphoreType.DMA(shape)
    any_spec = pl.BlockSpec(memory_space=pltpu.HBM)
    vmem_spec = pl.BlockSpec(memory_space=pltpu.VMEM)
    pairs = [2, 2, n_plane, n_plane, n_pos // FOLD - 1, n_pos // FOLD - 1, n_plane, n_plane]
    pairs += [n_pos - 1] * 4 + [n_plane] * 2
    combine, slots = pl.pallas_call(
        functools.partial(layer_kernel, n_pos, n_exp, chunk),
        out_shape=(
            jax.ShapeDtypeStruct((rows, n_slots), BF16),
            jax.ShapeDtypeStruct((n_slots, d), BF16),
        ),
        in_specs=[any_spec] * 5,
        out_specs=(vmem_spec, vmem_spec),
        scratch_shapes=[
            pltpu.VMEM((channels, periods, samples), BF16),
            pltpu.VMEM((rows, 3 * samples), BF16),
            pltpu.VMEM((3 * samples, d), BF16),
            pltpu.VMEM((n_slots, d), BF16),
            pltpu.VMEM((d, ff), BF16),
            pltpu.VMEM((ff, d), BF16),
            pltpu.VMEM((rows, d), BF16),
            pltpu.VMEM((2, 8, samples), F32),
            pltpu.VMEM((2, 8, samples), F32),
            pltpu.VMEM((n_exp, per, 128), F32),
            pltpu.VMEM((n_plane, per, 128), F32),
            pltpu.VMEM((n_pos // FOLD, per, 128), F32),
            pltpu.VMEM((FOLD, n_exp, per, half), F32),
            pltpu.VMEM((FOLD, n_exp) + packed, BF16),
            pltpu.VMEM((n_plane,) + packed, BF16),
            pltpu.VMEM((n_pos,) + packed, BF16),
            pltpu.VMEM((FOLD,) + packed, BF16),
            pltpu.VMEM((n_pos,) + packed, BF16),
            pltpu.VMEM((n_exp, FOLD) + packed, BF16),
            pltpu.VMEM((n_slots, d), F32),
            dma(4),
            dma(d // chunk),
        ]
        + [dma(c) for c in pairs],
        compiler_params=pltpu.CompilerParams(
            collective_id=0, has_side_effects=True, vmem_limit_bytes=63 * 2**20
        ),
        name="moe_layer",
    )(patches, conv_weight.reshape(3 * samples, d), phi.T, w_in, w_out)
    step = 32
    return pl.pallas_call(
        mix_kernel,
        grid=(channels // step,),
        out_shape=jax.ShapeDtypeStruct((channels, periods, d), BF16),
        in_specs=[
            pl.BlockSpec((step * periods, n_slots), lambda i: (i, 0)),
            pl.BlockSpec((n_slots, d), lambda i: (0, 0)),
        ],
        out_specs=pl.BlockSpec((step, periods, d), lambda i: (i, 0, 0)),
        compiler_params=pltpu.CompilerParams(vmem_limit_bytes=63 * 2**20),
        name="mix_slots",
    )(combine, slots)


def solution(mesh):
    in_specs = (
        P(("pos", "exp"), None, None),
        P(),
        P(),
        P("exp", None, "pos"),
        P("exp", "pos", None),
    )
    out_specs = P(("pos", "exp"), None, None)
    body = functools.partial(per_device, mesh.shape["pos"], mesh.shape["exp"])
    return jax.shard_map(
        body, mesh=mesh, in_specs=in_specs, out_specs=out_specs, check_vma=False
    )
```

```python
import functools

import jax
import jax.numpy as jnp
from jax import lax
from jax.experimental import pallas as pl
from jax.experimental.pallas import tpu as pltpu
from jax.sharding import PartitionSpec as P

MESH = pl.DeviceIdType.MESH
F32 = jnp.float32
BF16 = jnp.bfloat16
FOLD = 2


def pack(block):
    rows, width = block.shape
    if width % 256 == 0:
        half = width // 2
        return jnp.concatenate([block[:, :half], block[:, half:]], axis=0).astype(BF16)
    return jnp.concatenate([block, jnp.zeros_like(block)], axis=0).astype(BF16)


def packed_shape(rows, width):
    return (2 * rows, width // 2 if width % 256 == 0 else width)


def unpack(block, width):
    wide = block.astype(F32)
    rows = wide.shape[0] // 2
    if width % 256 == 0:
        return jnp.concatenate([wide[:rows], wide[rows:]], axis=1)
    return wide[:rows]


def layer_kernel(
    n_pos, n_exp, chunk,
    patches, taps, phi_t, w_in, w_out,
    combine_ref, slots_ref,
    x_raw, xs, xe, taps_v, phi_v, win_v, wout_v, tokens,
    halo_out, halo_in,
    stat_own, stat_plane, stat_z,
    sum_own, sum_out, sum_plane,
    in_all,
    term_out, term_pos,
    out_all, slots_v, combine_v,
    local_sem, chunk_sem,
    halo_s, halo_r, stat_es, stat_er, stat_ps, stat_pr,
    sum_s, sum_r, in_s, in_r, term_s, term_r,
    slot_s, slot_r,
):
    p, e = lax.axis_index("pos"), lax.axis_index("exp")
    count = n_pos * n_exp
    g = p * n_exp + e
    channels, periods, samples = x_raw.shape
    rows = channels * periods
    d = tokens.shape[1]
    n_slots = phi_v.shape[0]
    per = n_slots // n_exp
    half = d // FOLD
    n_chunks = d // chunk
    edge = rows // 8

    right, left = lax.rem(g + 1, count), lax.rem(g + count - 1, count)
    right_id = (right // n_exp, lax.rem(right, n_exp))
    left_id = (left // n_exp, lax.rem(left, n_exp))
    z, x = p // FOLD, lax.rem(p, FOLD)
    n_z = n_pos // FOLD
    plane = [(a, b) for a in reversed(range(FOLD)) for b in range(n_exp) if (a, b) != (0, 0)]
    plane_xe = [(lax.rem(x + a, FOLD), lax.rem(e + b, n_exp)) for a, b in plane]
    plane_ids = [(z * FOLD + a, b) for a, b in plane_xe]
    pos_p = [
        lax.rem(z + k, n_z) * FOLD + lax.rem(x + a, FOLD)
        for k in sorted(range(n_z), key=lambda k: k * (n_z - k) if k else n_z * n_z)
        for a in reversed(range(FOLD))
        if (k, a) != (0, 0)
    ]
    pos_ids = [(q, e) for q in pos_p]
    z_ids = [(lax.rem(z + k, n_z) * FOLD + x, e) for k in range(1, n_z)]

    barrier = pltpu.get_barrier_semaphore()
    for device in [right_id, left_id] + plane_ids + pos_ids:
        pl.semaphore_signal(barrier, inc=1, device_id=device, device_id_type=MESH)

    def send(src, dst, s, r, device):
        copy = pltpu.make_async_remote_copy(
            src_ref=src, dst_ref=dst, send_sem=s, recv_sem=r,
            device_id=device, device_id_type=MESH,
        )
        copy.start()
        return copy

    x_copy = pltpu.make_async_copy(patches, x_raw, local_sem.at[0])
    x_copy.start()

    def tap_copy(n):
        cols = pl.ds(pl.multiple_of(n * chunk, chunk), chunk)
        return pltpu.make_async_copy(taps.at[:, cols], taps_v.at[:, cols], chunk_sem.at[n])

    for n in range(n_chunks):
        tap_copy(n).start()
    phi_copy = pltpu.make_async_copy(phi_t, phi_v, local_sem.at[1])
    phi_copy.start()

    x_copy.wait()
    raw = x_raw[...].astype(F32).reshape(rows, samples)
    halo_out[0] = raw[rows - 8 :]
    halo_out[1] = raw[:8]
    xs[:, samples : 2 * samples] = raw.astype(BF16)
    up = pltpu.roll(raw, periods, 0)
    down = pltpu.roll(raw, rows - periods, 0)
    xs[:, :samples] = up.astype(BF16)
    xs[:, 2 * samples :] = down.astype(BF16)

    pl.semaphore_wait(barrier, 2 + len(plane_ids) + len(pos_ids))
    halo = [
        send(halo_out.at[0], halo_in.at[0], halo_s.at[0], halo_r.at[0], right_id),
        send(halo_out.at[1], halo_in.at[1], halo_s.at[1], halo_r.at[1], left_id),
    ]

    def encode(n, source):
        cols = pl.ds(pl.multiple_of(n * chunk, chunk), chunk)
        return cols, jnp.dot(source, taps_v[:, cols], preferred_element_type=F32).astype(BF16)

    @pl.loop(0, n_chunks)
    def _(n):
        tap_copy(n).wait()
        cols, value = encode(n, xs[edge : rows - edge])
        tokens[edge : rows - edge, cols] = value

    win_copy = pltpu.make_async_copy(w_in.at[0], win_v, local_sem.at[2])
    win_copy.start()
    wout_copy = pltpu.make_async_copy(w_out.at[0], wout_v, local_sem.at[3])
    wout_copy.start()

    for copy in halo:
        copy.wait()
    row16 = lax.broadcasted_iota(jnp.int32, (16, samples), 0)
    zero8 = jnp.zeros((8, samples), F32)
    before = jnp.concatenate([pltpu.roll(halo_in[0], 4, 0), zero8], axis=0)
    before = jnp.where(g == 0, 0.0, before)
    xs[0:16, :samples] = jnp.where(
        row16 < periods, before, xs[0:16, :samples].astype(F32)
    ).astype(BF16)
    after = jnp.concatenate([zero8, pltpu.roll(halo_in[1], 4, 0)], axis=0)
    after = jnp.where(g == count - 1, 0.0, after)
    xs[rows - 16 :, 2 * samples :] = jnp.where(
        row16 >= 16 - periods, after, xs[rows - 16 :, 2 * samples :].astype(F32)
    ).astype(BF16)

    xe[:edge] = xs[:edge]
    xe[edge:] = xs[rows - edge :]

    @pl.loop(0, n_chunks)
    def _(n):
        cols, value = encode(n, xe[...])
        tokens[:edge, cols] = value[:edge]
        tokens[rows - edge :, cols] = value[edge:]

    phi_copy.wait()
    contract_last = (((1,), (1,)), ((), ()))
    lt = lax.dot_general(phi_v[...], tokens[...], contract_last, preferred_element_type=F32)
    peak = jnp.max(lt, axis=1, keepdims=True)
    weights = jnp.exp(lt - peak)
    total = jnp.sum(weights, axis=1, keepdims=True)
    lane = lax.broadcasted_iota(jnp.int32, (n_slots, 128), 1)
    stats = jnp.where(lane < 64, peak, total)
    for q in range(n_exp):
        stat_own[q] = stats[q * per : (q + 1) * per]
    stat_copies = [
        send(stat_own.at[to[1]], stat_plane.at[k], stat_es.at[k], stat_er.at[k], to)
        for k, to in enumerate(plane_ids)
    ]
    sums = jnp.dot(weights.astype(BF16), tokens[...], preferred_element_type=F32)
    for q in range(n_exp):
        for f in range(FOLD):
            own = sums[q * per : (q + 1) * per, f * half : (f + 1) * half]
            sum_own[f, q] = own
            sum_out[f, q] = pack(own)
    sum_copies = [
        send(sum_out.at[a, b], sum_plane.at[k], sum_s.at[k], sum_r.at[k], to)
        for k, ((a, b), to) in enumerate(zip(plane_xe, plane_ids))
    ]

    def merge(blocks):
        peaks = [b[:, 0:1] for b in blocks]
        totals = [b[:, 64:65] for b in blocks]
        top = functools.reduce(jnp.maximum, peaks)
        scales = [jnp.exp(v - top) for v in peaks]
        whole = functools.reduce(jnp.add, [s * t for s, t in zip(scales, totals)])
        return top, scales, whole

    for copy in stat_copies:
        copy.wait()
    top_p, scales_p, total_p = merge(
        [stat_own[e]] + [stat_plane[k] for k in range(len(plane_ids))]
    )
    lane8 = lax.broadcasted_iota(jnp.int32, (per, 128), 1)
    stat_z[z] = jnp.where(lane8 < 64, top_p, total_p)
    z_copies = [
        send(stat_z.at[z], stat_z.at[z], stat_ps.at[k], stat_pr.at[k], to)
        for k, to in enumerate(z_ids)
    ]

    row_weights = jnp.exp(lt - jnp.max(lt, axis=0, keepdims=True))
    combine = row_weights / jnp.sum(row_weights, axis=0, keepdims=True)
    combine_v[...] = combine.T.astype(BF16)
    combine_copy = pltpu.make_async_copy(combine_v, combine_ref, local_sem.at[4])
    combine_copy.start()

    for copy in sum_copies:
        copy.wait()
    part = scales_p[0] * sum_own[x, e]
    for k in range(len(plane_ids)):
        part = part + scales_p[k + 1] * unpack(sum_plane[k], half)
    in_all[p] = pack(part)
    in_copies = [
        send(in_all.at[p], in_all.at[p], in_s.at[k], in_r.at[k], to)
        for k, to in enumerate(pos_ids)
    ]
    for copy in z_copies:
        copy.wait()
    top, scales_z, total_all = merge([stat_z[q] for q in range(n_z)])
    factors = [s / total_all for s in scales_z]
    win_copy.wait()
    for copy in in_copies:
        copy.wait()

    def gathered(f):
        terms = [factors[q] * unpack(in_all[q * FOLD + f], half) for q in range(n_z)]
        return functools.reduce(jnp.add, terms)

    slot_in = jnp.concatenate([gathered(f) for f in range(FOLD)], axis=1).astype(BF16)
    hidden = jax.nn.gelu(
        jnp.dot(slot_in, win_v[...], preferred_element_type=F32), approximate=True
    ).astype(BF16)
    wout_copy.wait()
    term = jnp.dot(hidden, wout_v[...], preferred_element_type=F32)
    for f in range(FOLD):
        term_out[f] = pack(term[:, f * half : (f + 1) * half])
    term_copies = [
        send(term_out.at[lax.rem(q, FOLD)], term_pos.at[p], term_s.at[k], term_r.at[k], to)
        for k, (q, to) in enumerate(zip(pos_p, pos_ids))
    ]
    term_pos[p] = term_out[x]
    for copy in term_copies:
        copy.wait()
    mine = functools.reduce(jnp.add, [unpack(term_pos[q], half) for q in range(n_pos)])
    out_all[e, x] = pack(mine)
    slot_copies = [
        send(out_all.at[e, x], out_all.at[e, x], slot_s.at[k], slot_r.at[k], to)
        for k, to in enumerate(plane_ids)
    ]
    combine_copy.wait()
    for copy in slot_copies:
        copy.wait()
    for i in range(n_exp):
        for f in range(FOLD):
            slots_v[i * per : (i + 1) * per, f * half : (f + 1) * half] = unpack(
                out_all[i, f], half
            )
    slots_ref[...] = slots_v[...].astype(BF16)


def mix_kernel(step, combine_ref, slots_ref, out_ref, out_v, sem):
    channels, periods, d = out_v.shape
    copies = []
    for i in range(channels // step):
        part = pl.ds(i * step, step)
        weights = combine_ref[i * step * periods : (i + 1) * step * periods]
        mixed = jnp.dot(weights, slots_ref[...], preferred_element_type=F32)
        out_v[part] = mixed.astype(BF16).reshape(step, periods, d)
        copy = pltpu.make_async_copy(out_v.at[part], out_ref.at[part], sem.at[i])
        copy.start()
        copies.append(copy)
    for copy in copies:
        copy.wait()


def per_device(n_pos, n_exp, patches, conv_weight, phi, w_in, w_out):
    channels, periods, samples = patches.shape
    rows = channels * periods
    d, n_slots = phi.shape
    ff = w_in.shape[2]
    per = n_slots // n_exp
    half = d // FOLD
    chunk = 1024
    packed = packed_shape(per, half)
    n_plane = n_exp * FOLD - 1
    dma = lambda *shape: pltpu.SemaphoreType.DMA(shape)
    any_spec = pl.BlockSpec(memory_space=pltpu.HBM)
    vmem_spec = pl.BlockSpec(memory_space=pltpu.VMEM)
    pairs = [2, 2, n_plane, n_plane, n_pos // FOLD - 1, n_pos // FOLD - 1, n_plane, n_plane]
    pairs += [n_pos - 1] * 4 + [n_plane] * 2
    combine, slots = pl.pallas_call(
        functools.partial(layer_kernel, n_pos, n_exp, chunk),
        out_shape=(
            jax.ShapeDtypeStruct((rows, n_slots), BF16),
            jax.ShapeDtypeStruct((n_slots, d), BF16),
        ),
        in_specs=[any_spec] * 5,
        out_specs=(any_spec, vmem_spec),
        scratch_shapes=[
            pltpu.VMEM((channels, periods, samples), BF16),
            pltpu.VMEM((rows, 3 * samples), BF16),
            pltpu.VMEM((rows // 4, 3 * samples), BF16),
            pltpu.VMEM((3 * samples, d), BF16),
            pltpu.VMEM((n_slots, d), BF16),
            pltpu.VMEM((d, ff), BF16),
            pltpu.VMEM((ff, d), BF16),
            pltpu.VMEM((rows, d), BF16),
            pltpu.VMEM((2, 8, samples), F32),
            pltpu.VMEM((2, 8, samples), F32),
            pltpu.VMEM((n_exp, per, 128), F32),
            pltpu.VMEM((n_plane, per, 128), F32),
            pltpu.VMEM((n_pos // FOLD, per, 128), F32),
            pltpu.VMEM((FOLD, n_exp, per, half), F32),
            pltpu.VMEM((FOLD, n_exp) + packed, BF16),
            pltpu.VMEM((n_plane,) + packed, BF16),
            pltpu.VMEM((n_pos,) + packed, BF16),
            pltpu.VMEM((FOLD,) + packed, BF16),
            pltpu.VMEM((n_pos,) + packed, BF16),
            pltpu.VMEM((n_exp, FOLD) + packed, BF16),
            pltpu.VMEM((n_slots, d), F32),
            pltpu.VMEM((rows, n_slots), BF16),
            dma(5),
            dma(d // chunk),
        ]
        + [dma(c) for c in pairs],
        compiler_params=pltpu.CompilerParams(
            collective_id=0, has_side_effects=True, vmem_limit_bytes=63 * 2**20
        ),
        name="moe_layer",
    )(patches, conv_weight.reshape(3 * samples, d), phi.T, w_in, w_out)
    step = 32
    return pl.pallas_call(
        functools.partial(mix_kernel, step),
        out_shape=jax.ShapeDtypeStruct((channels, periods, d), BF16),
        in_specs=[vmem_spec, vmem_spec],
        out_specs=any_spec,
        scratch_shapes=[pltpu.VMEM((channels, periods, d), BF16), dma(channels // step)],
        compiler_params=pltpu.CompilerParams(vmem_limit_bytes=63 * 2**20),
        name="mix_slots",
    )(combine, slots)


def solution(mesh):
    in_specs = (
        P(("pos", "exp"), None, None),
        P(),
        P(),
        P("exp", None, "pos"),
        P("exp", "pos", None),
    )
    out_specs = P(("pos", "exp"), None, None)
    body = functools.partial(per_device, mesh.shape["pos"], mesh.shape["exp"])
    return jax.shard_map(
        body, mesh=mesh, in_specs=in_specs, out_specs=out_specs, check_vma=False
    )
```
